32 devices in a mesh: group: 2 (over x), strike: 16 (over z, y, core).
Axes of the slice: x: 2, y: 2, z: 4, core: 2. Of those that a mesh axis runs over, the one named last changes fastest.
Arguments:
- pressure: float32 [128, 8, 512], P(('group', 'strike')), parts along dimension 0, may hold values from -4 to 4
- newton_step: float32 [128, 8, 512], P(('group', 'strike')), parts along dimension 0, may hold values from -4 to 4
- pore_volume: float32 [128, 8, 512], P(('group', 'strike')), parts along dimension 0, may hold values from 0.5 to 4
- old_mass: float32 [128, 8, 512], P(('group', 'strike')), parts along dimension 0, may hold values from 0.5 to 3
- trans_strike: float32 [128, 8, 512], P(('group', 'strike')), parts along dimension 0, may hold values from 0.05 to 1
- trans_layer: float32 [128, 8, 512], P(('group', 'strike')), parts along dimension 0, may hold values from 0.05 to 1
- trans_dip: float32 [128, 8, 512], P(('group', 'strike')), parts along dimension 0, may hold values from 0.05 to 1
- frac_pressure: float32 [32, 128, 128], P(('group', 'strike')), parts along dimension 0, may hold values from -4 to 4
- frac_step: float32 [32, 128, 128], P(('group', 'strike')), parts along dimension 0, may hold values from -4 to 4
- frac_volume: float32 [32, 128, 128], P(('group', 'strike')), parts along dimension 0, may hold values from 0.2 to 2
- frac_old_mass: float32 [32, 128, 128], P(('group', 'strike')), parts along dimension 0, may hold values from 0.2 to 2
- frac_trans_along: float32 [32, 128, 128], P(('group', 'strike')), parts along dimension 0, may hold values from 0.3 to 4
- frac_trans_across: float32 [32, 128, 128], P(('group', 'strike')), parts along dimension 0, may hold values from 0.3 to 4
- conn_count: int32 [32, 16], P(('group', 'strike')), parts along dimension 0, may hold values from 1 to 32, as said below
- conn_trans: float32 [32, 16, 32], P(('group', 'strike')), parts along dimension 0, may hold values from 0.1 to 2
- frac_index: int32 [32, 16, 32], P(('group', 'strike')), parts along dimension 0, may hold values from 0 to 16383
- matrix_index: int32 [32, 16, 32], P(('group', 'strike')), parts along dimension 0, may hold values from 0 to 16383
Outputs:
- matrix_residual: float32 [128, 8, 512], P(('group', 'strike')), parts along dimension 0
- matrix_product: float32 [128, 8, 512], P(('group', 'strike')), parts along dimension 0
- fracture_residual: float32 [32, 128, 128], P(('group', 'strike')), parts along dimension 0
- fracture_product: float32 [32, 128, 128], P(('group', 'strike')), parts along dimension 0
The draws below stay inside these ranges and needn't reach their ends.
There are 2 independent parts, one for each index of `group`. The reference program is written for one: setup_inputs(seed, part) draws one part's arguments, and reference() takes and returns one part's arrays. A program takes and returns all parts, laid end to end along the dimension named above; each array names one. Nothing has to cross between parts.
Inputs may be any that keep to these rules, and one draw needn't show every extreme that they name: In every part one strike index d is drawn for which conn_count[s, d] = 32 for every s; the other counts are even over the range.
All inputs are finite; a program needn't handle non-finite values.
Results may differ from the reference program's by a relative error of at most 0.0003.
Values sent between devices are 32-bit elements; how exact they have to be, the bound alone decides.
A program may use at most 64 MiB of HBM per device.

```python
import math
import jax
import jax.numpy as jnp
from jax import lax

NZL = 8
NY = 512
TILE = 128
CAP = 32
PEERS = 16
NX = 64
TILES = 16
M_DEV = 16384
FRAC_DEV = 16384


def draw_conn_count(key, part):
    key = jax.random.fold_in(key, 7)
    first_key, second_key = jax.random.split(key)
    hottest = jax.random.randint(first_key, (), 0, PEERS)
    counts = jax.random.randint(second_key, (PEERS, PEERS), 1, CAP + 1)
    columns = jnp.arange(PEERS)[None, :]
    return jnp.where(columns == hottest, CAP, counts).astype(jnp.int32)


def with_ends(values, own_key, low, largest):
    longest = values.shape.index(max(values.shape))
    spots = []
    for shift in (0, 1):
        where = [jax.random.randint(jax.random.fold_in(own_key, axis), (), 0, length) for axis, length in enumerate(values.shape)]
        where[longest] = (where[longest] + shift) % values.shape[longest]
        spots.append(tuple(where))
    return values.at[spots[0]].set(low).at[spots[1]].set(largest)


def block_scale(key, dims, pieces, least, top_value):
    gain = 1.0
    for dim, shards_of in pieces:
        heights = jax.random.uniform(jax.random.fold_in(jax.random.fold_in(key, 6), dim), (shards_of,), jnp.float32, least / len(pieces), top_value / len(pieces))
        gain = gain * jnp.repeat(jnp.exp(heights), dims[dim] // shards_of).reshape((-1,) + (1,) * (len(dims) - 1 - dim))
    return gain


def bell_draw(rng, dims, spread, limit, cuts=(), held_as=jnp.bfloat16):
    values = spread * jax.random.normal(rng, dims, jnp.float32)
    if cuts:
        values = values * block_scale(rng, dims, cuts, -0.22, 0.18)
    return jnp.clip(values, -limit, limit).astype(held_as)


def setup_inputs(seed: int = 0, part: int = 0) -> dict:
    key_of = jax.random.split(jax.random.key(seed), 18)
    part_splits = jax.random.split(jax.random.fold_in(key_of[17], part), 18)
    return {
        "pressure": bell_draw(part_splits[0], (NX, NZL, NY), 1.0, 4.0, ((0, 16),), jnp.float32),
        "newton_step": bell_draw(part_splits[1], (NX, NZL, NY), 1.0, 4.0, ((0, 16),), jnp.float32),
        "pore_volume": jnp.clip(jnp.exp(math.log(4.0) - 2.0794415 * jax.random.uniform(part_splits[2], (NX, NZL, NY), jnp.float32) ** block_scale(part_splits[2], (NX, NZL, NY), ((0, 16),), -0.2, 0.2)), 0.5, 4.0),
        "old_mass": jnp.clip(0.5 + 2.5 * jax.random.uniform(part_splits[3], (NX, NZL, NY), jnp.float32) ** block_scale(part_splits[3], (NX, NZL, NY), ((0, 16),), -0.2, 0.2), 0.5, 3.0),
        "trans_strike": jnp.clip(jnp.exp(math.log(1.0) - 2.9957323 * jax.random.uniform(part_splits[4], (NX, NZL, NY), jnp.float32) ** block_scale(part_splits[4], (NX, NZL, NY), ((0, 16),), -0.2, 0.2)), 0.05, 1.0),
        "trans_layer": jnp.clip(jnp.exp(math.log(1.0) - 2.9957323 * jax.random.uniform(part_splits[5], (NX, NZL, NY), jnp.float32) ** block_scale(part_splits[5], (NX, NZL, NY), ((0, 16),), -0.2, 0.2)), 0.05, 1.0),
        "trans_dip": jnp.clip(jnp.exp(math.log(1.0) - 2.9957323 * jax.random.uniform(part_splits[6], (NX, NZL, NY), jnp.float32) ** block_scale(part_splits[6], (NX, NZL, NY), ((0, 16),), -0.2, 0.2)), 0.05, 1.0),
        "frac_pressure": bell_draw(part_splits[7], (TILES, TILE, TILE), 1.0, 4.0, ((0, 16),), jnp.float32),
        "frac_step": bell_draw(part_splits[8], (TILES, TILE, TILE), 1.0, 4.0, ((0, 16),), jnp.float32),
        "frac_volume": jnp.clip(jnp.exp(math.log(2.0) - 2.3025851 * jax.random.uniform(part_splits[9], (TILES, TILE, TILE), jnp.float32) ** block_scale(part_splits[9], (TILES, TILE, TILE), ((0, 16),), -0.2, 0.2)), 0.2, 2.0),
        "frac_old_mass": jnp.clip(0.2 + 1.8 * jax.random.uniform(part_splits[10], (TILES, TILE, TILE), jnp.float32) ** block_scale(part_splits[10], (TILES, TILE, TILE), ((0, 16),), -0.2, 0.2), 0.2, 2.0),
        "frac_trans_along": jnp.clip(jnp.exp(math.log(4.0) - 2.5902671 * jax.random.uniform(part_splits[11], (TILES, TILE, TILE), jnp.float32) ** block_scale(part_splits[11], (TILES, TILE, TILE), ((0, 16),), -0.2, 0.2)), 0.3, 4.0),
        "frac_trans_across": jnp.clip(jnp.exp(math.log(4.0) - 2.5902671 * jax.random.uniform(part_splits[12], (TILES, TILE, TILE), jnp.float32) ** block_scale(part_splits[12], (TILES, TILE, TILE), ((0, 16),), -0.2, 0.2)), 0.3, 4.0),
        "conn_count": draw_conn_count(jax.random.fold_in(jax.random.fold_in(key_of[17], part), 71), part),
        "conn_trans": jnp.clip(jnp.exp(math.log(2.0) - 2.9957323 * jax.random.uniform(part_splits[14], (PEERS, PEERS, CAP), jnp.float32) ** block_scale(part_splits[14], (PEERS, PEERS, CAP), ((0, 16),), -0.2, 0.2)), 0.1, 2.0),
        "frac_index": with_ends(jax.random.randint(part_splits[15], (PEERS, PEERS, CAP), 0, FRAC_DEV), jax.random.fold_in(part_splits[15], 1), 0, FRAC_DEV - 1).astype(jnp.int32),
        "matrix_index": with_ends(jax.random.randint(part_splits[16], (PEERS, PEERS, CAP), 0, min(M_DEV, 32768)), jax.random.fold_in(part_splits[16], 1), 0, (min(M_DEV, 32768)) - 1).astype(jnp.int32),
    }


COMPRESSIBILITY = 0.5


def face_flux(trans_face, left_press, right_press, left_delta, right_delta):
    left_rho = jnp.exp(COMPRESSIBILITY * left_press)
    right_rho = jnp.exp(COMPRESSIBILITY * right_press)
    average = 0.5 * (left_rho + right_rho)
    drop = left_press - right_press
    flux = trans_face * average * drop
    tangent = trans_face * (0.5 * COMPRESSIBILITY * (left_rho * left_delta + right_rho * right_delta) * drop + average * (left_delta - right_delta))
    return flux, tangent


def lower_part(array, dim_index):
    return lax.slice_in_dim(array, 0, array.shape[dim_index] - 1, axis=dim_index)


def upper_part(array, dim_index):
    return lax.slice_in_dim(array, 1, array.shape[dim_index], axis=dim_index)


def add_faces(resid, linear, press, delta, trans, dim_index):
    flux, tangent = face_flux(lower_part(trans, dim_index), lower_part(press, dim_index), upper_part(press, dim_index), lower_part(delta, dim_index), upper_part(delta, dim_index))
    after = tuple((0, 1) if position == dim_index else (0, 0) for position in range(press.ndim))
    before = tuple((1, 0) if position == dim_index else (0, 0) for position in range(press.ndim))
    resid = resid + jnp.pad(flux, after) - jnp.pad(flux, before)
    linear = linear + jnp.pad(tangent, after) - jnp.pad(tangent, before)
    return resid, linear


def accumulate(press, delta, volume, old):
    rho_now = jnp.exp(COMPRESSIBILITY * press)
    return volume * rho_now - old, volume * COMPRESSIBILITY * rho_now * delta


def reference(pressure, newton_step, pore_volume, old_mass, trans_strike, trans_layer, trans_dip, frac_pressure, frac_step, frac_volume, frac_old_mass, frac_trans_along, frac_trans_across, conn_count, conn_trans, frac_index, matrix_index):
    resid, linear = accumulate(pressure, newton_step, pore_volume, old_mass)
    for dim_index, trans in ((0, trans_strike), (1, trans_layer), (2, trans_dip)):
        resid, linear = add_faces(resid, linear, pressure, newton_step, trans, dim_index)
    frac_resid, frac_linear = accumulate(frac_pressure, frac_step, frac_volume, frac_old_mass)
    for dim_index, trans in ((1, frac_trans_along), (2, frac_trans_across)):
        frac_resid, frac_linear = add_faces(frac_resid, frac_linear, frac_pressure, frac_step, trans, dim_index)
    sources = jnp.broadcast_to(jnp.arange(PEERS, dtype=jnp.int32)[:, None, None], frac_index.shape)
    targets = jnp.broadcast_to(jnp.arange(PEERS, dtype=jnp.int32)[None, :, None], frac_index.shape)
    slots = jnp.arange(CAP, dtype=jnp.int32)[None, None, :]
    live_trans = jnp.where(slots < conn_count[:, :, None], conn_trans, jnp.zeros_like(conn_trans))
    matrix_cells = jnp.transpose(matrix_index, (1, 0, 2))
    frac_press = frac_pressure.reshape(PEERS, -1)[sources, frac_index]
    frac_delta = frac_step.reshape(PEERS, -1)[sources, frac_index]
    matrix_press = pressure.reshape(PEERS, -1)[targets, matrix_cells]
    matrix_delta = newton_step.reshape(PEERS, -1)[targets, matrix_cells]
    flux, tangent = face_flux(live_trans, matrix_press, frac_press, matrix_delta, frac_delta)
    resid = resid.reshape(PEERS, -1).at[targets, matrix_cells].add(flux).reshape(pressure.shape)
    linear = linear.reshape(PEERS, -1).at[targets, matrix_cells].add(tangent).reshape(pressure.shape)
    frac_resid = frac_resid.reshape(PEERS, -1).at[sources, frac_index].add(-flux).reshape(frac_pressure.shape)
    frac_linear = frac_linear.reshape(PEERS, -1).at[sources, frac_index].add(-tangent).reshape(frac_pressure.shape)
    return resid, linear, frac_resid, frac_linear
```

```python
import functools

import jax
import jax.numpy as jnp
from jax import lax
from jax.experimental import pallas as pl
from jax.experimental.pallas import tpu as pltpu
from jax.sharding import PartitionSpec as P

COMPRESSIBILITY = 0.5
LANES = 128
MESH = pl.DeviceIdType.MESH


def face(trans, pa, pb, da, db, ea, eb, ga, gb):
    drop = pa - pb
    total = 0.5 * trans * (ea + eb)
    flux = total * drop
    tangent = (0.25 * trans) * (ga + gb) * drop + total * (da - db)
    return flux, tangent


def shift_faces(resid, linear, trans, p, d, e, g, axis):
    size = p.shape[axis]
    here = lax.broadcasted_iota(jnp.int32, p.shape, axis)
    trans = jnp.where(here < size - 1, trans, 0.0)
    up = lambda x: pltpu.roll(x, size - 1, axis)
    down = lambda x: pltpu.roll(x, 1, axis)
    flux, tangent = face(trans, p, up(p), d, up(d), e, up(e), g, up(g))
    return resid + flux - down(flux), linear + tangent - down(tangent)


def split(x, terms):
    out = []
    for _ in range(terms):
        head = x.astype(jnp.bfloat16)
        out.append(head)
        x = x - head.astype(jnp.float32)
    return out


def pack(x):
    fold = LANES // x.shape[1]
    n = x.shape[0] // fold
    return jnp.concatenate([x[b * n : (b + 1) * n] for b in range(fold)], axis=1)


def unpack(x, width):
    fold = LANES // width
    return jnp.concatenate([x[:, b * width : (b + 1) * width] for b in range(fold)], axis=0)


def wide(rows, ref_rows):
    iota = lax.broadcasted_iota(jnp.int32, (ref_rows, LANES), 0)
    return [iota == rows[a : a + 1, :] for a in range(rows.shape[0])]


def ones_of(masks):
    return jnp.concatenate(
        [jnp.where(m, 1.0, 0.0).astype(jnp.bfloat16) for m in masks], axis=1
    )


def gather(first, second, row_masks, col_ones):
    size = first.shape[0]
    lhs = jnp.concatenate(
        [jnp.concatenate(split(x, 3), axis=1) for x in (first, second)], axis=0
    )
    rhs = jnp.concatenate([col_ones] * 3, axis=0)
    found = jnp.dot(lhs, rhs, preferred_element_type=jnp.float32)
    out = []
    for q in range(2):
        rows = []
        for a, mask in enumerate(row_masks):
            block = found[q * size : (q + 1) * size, a * LANES : (a + 1) * LANES]
            rows.append(jnp.sum(jnp.where(mask, block, 0.0), axis=0, keepdims=True))
        out.append(jnp.concatenate(rows, axis=0))
    return out


def scatter(first, second, row_ones, col_masks):
    def weights(part):
        stacked = []
        for rows in part:
            stacked.append(
                jnp.concatenate(
                    [
                        jnp.where(mask, rows[a : a + 1, :].astype(jnp.float32), 0.0).astype(
                            jnp.bfloat16
                        )
                        for a, mask in enumerate(col_masks)
                    ],
                    axis=1,
                )
            )
        return jnp.concatenate(stacked, axis=1)

    rhs = jnp.concatenate([weights(split(first, 2)), weights(split(second, 2))], axis=0)
    lhs = jnp.concatenate([row_ones] * 2, axis=1)
    sums = lax.dot_general(
        lhs, rhs, (((1,), (1,)), ((), ())), preferred_element_type=jnp.float32
    )
    return sums[:, :LANES], sums[:, LANES:]


def kernel(peers, *refs):
    ins, outs, scratch = refs[:17], refs[17:21], refs[21:]
    bufs = scratch[:17]
    send, recv, low, high, load_sem, send_sem, recv_sem, halo_send, halo_recv = scratch[17:]
    me = lax.axis_index("strike")
    load = [
        pltpu.make_async_copy(ins[i], bufs[i], load_sem.at[i]) for i in range(17)
    ]
    order = (16, 15, 0, 1, 7, 8, 13, 14, 2, 3, 4, 5, 6, 9, 10, 11, 12)
    for i in order:
        load[i].start()

    barrier = pltpu.get_barrier_semaphore()

    def greet(off, carry):
        pl.semaphore_signal(
            barrier, 1, device_id={"strike": lax.rem(me + off, peers)}, device_id_type=MESH
        )
        return carry

    lax.fori_loop(1, peers, greet, 0, unroll=peers <= 16)

    (press, step, pore, old, t_strike, t_layer, t_dip) = bufs[:7]
    (f_press, f_step, f_volume, f_old, f_along, f_across) = bufs[7:13]
    count, c_trans, f_index, m_index = bufs[13:]
    nx, nz, ny = press.shape
    side = f_press.shape[1]
    rows_m = nx * nz
    cols = ny // LANES
    cap = c_trans.shape[2]

    def fold(x):
        flat = x.reshape(rows_m, ny)
        return jnp.concatenate(
            [flat[:, j * LANES : (j + 1) * LANES] for j in range(cols)], axis=0
        )

    def unfold(x):
        flat = jnp.concatenate(
            [x[j * rows_m : (j + 1) * rows_m] for j in range(cols)], axis=1
        )
        return flat.reshape(nx, nz, ny)

    for i in (16, 0, 1):
        load[i].wait()
    cell = pack(m_index[0])
    along = cell & (ny - 1)
    m_row = (along >> 7) * rows_m + (cell >> (ny.bit_length() - 1))
    m_col = along & (LANES - 1)
    m_row_masks = wide(m_row, rows_m * cols)
    m_col_masks = wide(m_col, LANES)
    mp, md = gather(fold(press[...]), fold(step[...]), m_row_masks, ones_of(m_col_masks))
    mp, md = unpack(mp, cap), unpack(md, cap)

    for i in (15, 7, 8):
        load[i].wait()
    cell = pack(f_index[0])
    f_row = cell >> 7
    f_col = cell & (LANES - 1)
    f_row_masks = wide(f_row, side)
    f_col_masks = wide(f_col, LANES)
    fp, fd = gather(f_press[0], f_step[0], f_row_masks, ones_of(f_col_masks))
    fp, fd = unpack(fp, cap), unpack(fd, cap)

    for i in (13, 14):
        load[i].wait()
    diagonal = lax.broadcasted_iota(jnp.int32, (peers, peers), 0) == lax.broadcasted_iota(
        jnp.int32, (peers, peers), 1
    )
    limit = jnp.sum(
        jnp.where(diagonal, count[...].astype(jnp.float32), 0.0), axis=1, keepdims=True
    )
    slot = lax.broadcasted_iota(jnp.int32, (peers, cap), 1).astype(jnp.float32)
    tr = jnp.where(slot < limit, c_trans[0], 0.0)

    first = jnp.concatenate([fp, fd, tr, mp], axis=1)
    send[:, 0, :] = first
    send[:, 1, :] = jnp.concatenate([md, jnp.zeros((peers, LANES - cap), jnp.float32)], axis=1)

    pl.semaphore_wait(barrier, peers - 1)

    def exchange(off, to, slot_there):
        return pltpu.make_async_remote_copy(
            src_ref=send.at[to],
            dst_ref=recv.at[slot_there],
            send_sem=send_sem.at[off],
            recv_sem=recv_sem.at[off],
            device_id={"strike": to},
            device_id_type=MESH,
        )

    def push(off, carry):
        exchange(off, lax.rem(me + off, peers), me).start()
        return carry

    lax.fori_loop(1, peers, push, 0, unroll=peers <= 16)

    following = lax.rem(me + 1, peers)
    previous = lax.rem(me + peers - 1, peers)

    load[4].wait()
    upward = [
        pltpu.make_async_remote_copy(
            src_ref=x.at[nx - 1],
            dst_ref=low.at[i],
            send_sem=halo_send.at[i],
            recv_sem=halo_recv.at[i],
            device_id={"strike": following},
            device_id_type=MESH,
        )
        for i, x in enumerate((press, step, t_strike))
    ]
    downward = [
        pltpu.make_async_remote_copy(
            src_ref=x.at[0],
            dst_ref=high.at[i],
            send_sem=halo_send.at[3 + i],
            recv_sem=halo_recv.at[3 + i],
            device_id={"strike": previous},
            device_id_type=MESH,
        )
        for i, x in enumerate((press, step))
    ]

    @pl.when(me < peers - 1)
    def _():
        for copy in upward:
            copy.start()

    @pl.when(me > 0)
    def _():
        for copy in downward:
            copy.start()

    recv[me] = send[me]

    for i in (2, 3, 5, 6, 9, 10, 11, 12):
        load[i].wait()

    out_mr, out_mp, out_fr, out_fp = outs
    p, d = press[...], step[...]
    e = jnp.exp(COMPRESSIBILITY * p)
    g = e * d
    resid = pore[...] * e - old[...]
    linear = pore[...] * COMPRESSIBILITY * g
    for axis, trans in ((1, t_layer), (2, t_dip)):
        resid, linear = shift_faces(resid, linear, trans[...], p, d, e, g, axis)
    planes_r = [resid[i] for i in range(nx)]
    planes_l = [linear[i] for i in range(nx)]
    for i in range(nx - 1):
        flux, tangent = face(
            t_strike[i], p[i], p[i + 1], d[i], d[i + 1], e[i], e[i + 1], g[i], g[i + 1]
        )
        planes_r[i] = planes_r[i] + flux
        planes_l[i] = planes_l[i] + tangent
        planes_r[i + 1] = planes_r[i + 1] - flux
        planes_l[i + 1] = planes_l[i + 1] - tangent
    for i in range(nx):
        out_mr[i] = planes_r[i]
        out_mp[i] = planes_l[i]

    q, w = f_press[0], f_step[0]
    h = jnp.exp(COMPRESSIBILITY * q)
    k = h * w
    f_resid = f_volume[0] * h - f_old[0]
    f_linear = f_volume[0] * COMPRESSIBILITY * k
    for axis, trans in ((0, f_along), (1, f_across)):
        f_resid, f_linear = shift_faces(f_resid, f_linear, trans[0], q, w, h, k, axis)
    out_fr[0] = f_resid
    out_fp[0] = f_linear

    def edge(trans, a, b):
        return face(
            trans,
            a[0],
            b[0],
            a[1],
            b[1],
            jnp.exp(COMPRESSIBILITY * a[0]),
            jnp.exp(COMPRESSIBILITY * b[0]),
            jnp.exp(COMPRESSIBILITY * a[0]) * a[1],
            jnp.exp(COMPRESSIBILITY * b[0]) * b[1],
        )

    @pl.when(me > 0)
    def _():
        for copy in upward:
            copy.wait_recv()
        flux, tangent = edge(low[2], (low[0], low[1]), (press[0], step[0]))
        out_mr[0] = out_mr[0] - flux
        out_mp[0] = out_mp[0] - tangent

    @pl.when(me < peers - 1)
    def _():
        for copy in downward:
            copy.wait_recv()
        flux, tangent = edge(
            t_strike[nx - 1], (press[nx - 1], step[nx - 1]), (high[0], high[1])
        )
        out_mr[nx - 1] = out_mr[nx - 1] + flux
        out_mp[nx - 1] = out_mp[nx - 1] + tangent

    def take(off, carry):
        exchange(off, lax.rem(me + off, peers), lax.rem(me + peers - off, peers)).wait_recv()
        return carry

    lax.fori_loop(1, peers, take, 0, unroll=peers <= 16)

    got = recv[:, 0, :]
    got_fp, got_fd, got_tr, got_mp = (got[:, i * cap : (i + 1) * cap] for i in range(4))
    got_md = recv[:, 1, 0:cap]

    def link(trans, a, b):
        ea, eb = jnp.exp(COMPRESSIBILITY * a[0]), jnp.exp(COMPRESSIBILITY * b[0])
        return face(trans, a[0], b[0], a[1], b[1], ea, eb, ea * a[1], eb * b[1])

    m_flux, m_tangent = link(got_tr, (mp, md), (got_fp, got_fd))
    sums = scatter(pack(m_flux), pack(m_tangent), ones_of(m_row_masks), m_col_masks)
    out_mr[...] += unfold(sums[0])
    out_mp[...] += unfold(sums[1])
    f_flux, f_tangent = link(tr, (got_mp, got_md), (fp, fd))
    sums = scatter(pack(f_flux), pack(f_tangent), ones_of(f_row_masks), f_col_masks)
    out_fr[0] -= sums[0]
    out_fp[0] -= sums[1]

    def sent(off, carry):
        exchange(off, lax.rem(me + off, peers), me).wait_send()
        return carry

    lax.fori_loop(1, peers, sent, 0, unroll=peers <= 16)

    @pl.when(me < peers - 1)
    def _():
        for copy in upward:
            copy.wait_send()

    @pl.when(me > 0)
    def _():
        for copy in downward:
            copy.wait_send()


def per_device(peers, *args):
    nx, nz, ny = args[0].shape
    outs = [jax.ShapeDtypeStruct(args[i].shape, jnp.float32) for i in (0, 0, 7, 7)]
    return pl.pallas_call(
        functools.partial(kernel, peers),
        out_shape=outs,
        in_specs=[pl.BlockSpec(memory_space=pl.ANY)] * 17,
        out_specs=[pl.BlockSpec(memory_space=pltpu.VMEM)] * 4,
        scratch_shapes=[pltpu.VMEM(x.shape, x.dtype) for x in args]
        + [
            pltpu.VMEM((peers, 2, LANES), jnp.float32),
            pltpu.VMEM((peers, 2, LANES), jnp.float32),
            pltpu.VMEM((3, nz, ny), jnp.float32),
            pltpu.VMEM((2, nz, ny), jnp.float32),
            pltpu.SemaphoreType.DMA((17,)),
            pltpu.SemaphoreType.DMA((peers,)),
            pltpu.SemaphoreType.DMA((peers,)),
            pltpu.SemaphoreType.DMA((5,)),
            pltpu.SemaphoreType.DMA((5,)),
        ],
        compiler_params=pltpu.CompilerParams(
            collective_id=0, has_side_effects=True, vmem_limit_bytes=32 * 1024 * 1024
        ),
    )(*args)


def solution(mesh):
    three = P(("group", "strike"), None, None)
    two = P(("group", "strike"), None)
    return jax.shard_map(
        functools.partial(per_device, mesh.shape["strike"]),
        mesh=mesh,
        in_specs=(three,) * 13 + (two,) + (three,) * 3,
        out_specs=(three,) * 4,
        check_vma=False,
    )
```

```python
import functools

import jax
import jax.numpy as jnp
from jax import lax
from jax.experimental import pallas as pl
from jax.experimental.pallas import tpu as pltpu
from jax.sharding import PartitionSpec as P

COMPRESSIBILITY = 0.5
LANES = 128
MESH = pl.DeviceIdType.MESH


def face(trans, pa, pb, da, db, ea, eb, ga, gb):
    drop = pa - pb
    total = 0.5 * trans * (ea + eb)
    flux = total * drop
    tangent = (0.25 * trans) * (ga + gb) * drop + total * (da - db)
    return flux, tangent


def shift_faces(resid, linear, trans, p, d, e, g, axis):
    size = p.shape[axis]
    here = lax.broadcasted_iota(jnp.int32, p.shape, axis)
    trans = jnp.where(here < size - 1, trans, 0.0)
    up = lambda x: pltpu.roll(x, size - 1, axis)
    down = lambda x: pltpu.roll(x, 1, axis)
    flux, tangent = face(trans, p, up(p), d, up(d), e, up(e), g, up(g))
    return resid + flux - down(flux), linear + tangent - down(tangent)


def split(x, terms):
    out = []
    for _ in range(terms):
        head = x.astype(jnp.bfloat16)
        out.append(head)
        x = x - head.astype(jnp.float32)
    return out


def pack(x):
    fold = LANES // x.shape[1]
    n = x.shape[0] // fold
    return jnp.concatenate([x[b * n : (b + 1) * n] for b in range(fold)], axis=1)


def unpack(x, width):
    fold = LANES // width
    return jnp.concatenate([x[:, b * width : (b + 1) * width] for b in range(fold)], axis=0)


def wide(rows, ref_rows):
    iota = lax.broadcasted_iota(jnp.int32, (ref_rows, LANES), 0)
    return [iota == rows[a : a + 1, :] for a in range(rows.shape[0])]


def ones_of(masks):
    return jnp.concatenate(
        [jnp.where(m, 1.0, 0.0).astype(jnp.bfloat16) for m in masks], axis=1
    )


def gather(first, second, row_masks, col_ones):
    size = first.shape[0]
    lhs = jnp.concatenate(
        [jnp.concatenate(split(x, 3), axis=1) for x in (first, second)], axis=0
    )
    rhs = jnp.concatenate([col_ones] * 3, axis=0)
    found = jnp.dot(lhs, rhs, preferred_element_type=jnp.float32)
    out = []
    for q in range(2):
        rows = []
        for a, mask in enumerate(row_masks):
            block = found[q * size : (q + 1) * size, a * LANES : (a + 1) * LANES]
            rows.append(jnp.sum(jnp.where(mask, block, 0.0), axis=0, keepdims=True))
        out.append(jnp.concatenate(rows, axis=0))
    return out


def scatter(first, second, row_ones, col_masks):
    def weights(part):
        stacked = []
        for rows in part:
            stacked.append(
                jnp.concatenate(
                    [
                        jnp.where(mask, rows[a : a + 1, :].astype(jnp.float32), 0.0).astype(
                            jnp.bfloat16
                        )
                        for a, mask in enumerate(col_masks)
                    ],
                    axis=1,
                )
            )
        return jnp.concatenate(stacked, axis=1)

    rhs = jnp.concatenate([weights(split(first, 2)), weights(split(second, 2))], axis=0)
    lhs = jnp.concatenate([row_ones] * 2, axis=1)
    sums = lax.dot_general(
        lhs, rhs, (((1,), (1,)), ((), ())), preferred_element_type=jnp.float32
    )
    return sums[:, :LANES], sums[:, LANES:]


def store(*refs):
    n = (len(refs) - 1) // 2
    copies = [
        pltpu.make_async_copy(refs[i], refs[n + i], refs[-1].at[i]) for i in range(n)
    ]
    for copy in copies:
        copy.start()
    for copy in copies:
        copy.wait()


def kernel(peers, *refs):
    ins, outs, scratch = refs[:17], refs[17:21], refs[21:]
    bufs = scratch[:17]
    send, recv, low, high, load_sem, send_sem, recv_sem, halo_send, halo_recv = scratch[17:]
    me = lax.axis_index("strike")
    load = [
        pltpu.make_async_copy(ins[i], bufs[i], load_sem.at[i]) for i in range(17)
    ]
    order = (16, 15, 0, 1, 7, 8, 13, 14, 2, 3, 4, 5, 6, 9, 10, 11, 12)
    for i in order:
        load[i].start()

    barrier = pltpu.get_barrier_semaphore()

    def greet(off, carry):
        pl.semaphore_signal(
            barrier, 1, device_id={"strike": lax.rem(me + off, peers)}, device_id_type=MESH
        )
        return carry

    lax.fori_loop(1, peers, greet, 0, unroll=peers <= 16)

    (press, step, pore, old, t_strike, t_layer, t_dip) = bufs[:7]
    (f_press, f_step, f_volume, f_old, f_along, f_across) = bufs[7:13]
    count, c_trans, f_index, m_index = bufs[13:]
    nx, nz, ny = press.shape
    side = f_press.shape[1]
    rows_m = nx * nz
    cols = ny // LANES
    cap = c_trans.shape[2]

    def fold(x):
        flat = x.reshape(rows_m, ny)
        return jnp.concatenate(
            [flat[:, j * LANES : (j + 1) * LANES] for j in range(cols)], axis=0
        )

    def unfold(x):
        flat = jnp.concatenate(
            [x[j * rows_m : (j + 1) * rows_m] for j in range(cols)], axis=1
        )
        return flat.reshape(nx, nz, ny)

    for i in (16, 0, 1):
        load[i].wait()
    cell = pack(m_index[0])
    along = cell & (ny - 1)
    m_row = (along >> 7) * rows_m + (cell >> (ny.bit_length() - 1))
    m_col = along & (LANES - 1)
    m_row_masks = wide(m_row, rows_m * cols)
    m_col_masks = wide(m_col, LANES)
    mp, md = gather(fold(press[...]), fold(step[...]), m_row_masks, ones_of(m_col_masks))
    mp, md = unpack(mp, cap), unpack(md, cap)

    for i in (15, 7, 8):
        load[i].wait()
    cell = pack(f_index[0])
    f_row = cell >> 7
    f_col = cell & (LANES - 1)
    f_row_masks = wide(f_row, side)
    f_col_masks = wide(f_col, LANES)
    fp, fd = gather(f_press[0], f_step[0], f_row_masks, ones_of(f_col_masks))
    fp, fd = unpack(fp, cap), unpack(fd, cap)

    for i in (13, 14):
        load[i].wait()
    diagonal = lax.broadcasted_iota(jnp.int32, (peers, peers), 0) == lax.broadcasted_iota(
        jnp.int32, (peers, peers), 1
    )
    limit = jnp.sum(
        jnp.where(diagonal, count[...].astype(jnp.float32), 0.0), axis=1, keepdims=True
    )
    slot = lax.broadcasted_iota(jnp.int32, (peers, cap), 1).astype(jnp.float32)
    tr = jnp.where(slot < limit, c_trans[0], 0.0)

    first = jnp.concatenate([fp, fd, tr, mp], axis=1)
    send[:, 0, :] = first
    send[:, 1, :] = jnp.concatenate([md, jnp.zeros((peers, LANES - cap), jnp.float32)], axis=1)

    pl.semaphore_wait(barrier, peers - 1)

    def exchange(off, to, slot_there):
        return pltpu.make_async_remote_copy(
            src_ref=send.at[to],
            dst_ref=recv.at[slot_there],
            send_sem=send_sem.at[off],
            recv_sem=recv_sem.at[off],
            device_id={"strike": to},
            device_id_type=MESH,
        )

    def push(off, carry):
        exchange(off, lax.rem(me + off, peers), me).start()
        return carry

    lax.fori_loop(1, peers, push, 0, unroll=peers <= 16)

    following = lax.rem(me + 1, peers)
    previous = lax.rem(me + peers - 1, peers)

    load[4].wait()
    upward = [
        pltpu.make_async_remote_copy(
            src_ref=x.at[nx - 1],
            dst_ref=low.at[i],
            send_sem=halo_send.at[i],
            recv_sem=halo_recv.at[i],
            device_id={"strike": following},
            device_id_type=MESH,
        )
        for i, x in enumerate((press, step, t_strike))
    ]
    downward = [
        pltpu.make_async_remote_copy(
            src_ref=x.at[0],
            dst_ref=high.at[i],
            send_sem=halo_send.at[3 + i],
            recv_sem=halo_recv.at[3 + i],
            device_id={"strike": previous},
            device_id_type=MESH,
        )
        for i, x in enumerate((press, step))
    ]

    @pl.when(me < peers - 1)
    def _():
        for copy in upward:
            copy.start()

    @pl.when(me > 0)
    def _():
        for copy in downward:
            copy.start()

    recv[me] = send[me]

    for i in (2, 3, 5, 6, 9, 10, 11, 12):
        load[i].wait()

    out_mr, out_mp, out_fr, out_fp = outs
    p, d = press[...], step[...]
    e = jnp.exp(COMPRESSIBILITY * p)
    g = e * d
    resid = pore[...] * e - old[...]
    linear = pore[...] * COMPRESSIBILITY * g
    for axis, trans in ((1, t_layer), (2, t_dip)):
        resid, linear = shift_faces(resid, linear, trans[...], p, d, e, g, axis)
    planes_r = [resid[i] for i in range(nx)]
    planes_l = [linear[i] for i in range(nx)]
    for i in range(nx - 1):
        flux, tangent = face(
            t_strike[i], p[i], p[i + 1], d[i], d[i + 1], e[i], e[i + 1], g[i], g[i + 1]
        )
        planes_r[i] = planes_r[i] + flux
        planes_l[i] = planes_l[i] + tangent
        planes_r[i + 1] = planes_r[i + 1] - flux
        planes_l[i + 1] = planes_l[i + 1] - tangent
    for i in range(nx):
        out_mr[i] = planes_r[i]
        out_mp[i] = planes_l[i]

    q, w = f_press[0], f_step[0]
    h = jnp.exp(COMPRESSIBILITY * q)
    k = h * w
    f_resid = f_volume[0] * h - f_old[0]
    f_linear = f_volume[0] * COMPRESSIBILITY * k
    for axis, trans in ((0, f_along), (1, f_across)):
        f_resid, f_linear = shift_faces(f_resid, f_linear, trans[0], q, w, h, k, axis)
    out_fr[0] = f_resid
    out_fp[0] = f_linear

    def edge(trans, a, b):
        return face(
            trans,
            a[0],
            b[0],
            a[1],
            b[1],
            jnp.exp(COMPRESSIBILITY * a[0]),
            jnp.exp(COMPRESSIBILITY * b[0]),
            jnp.exp(COMPRESSIBILITY * a[0]) * a[1],
            jnp.exp(COMPRESSIBILITY * b[0]) * b[1],
        )

    @pl.when(me > 0)
    def _():
        for copy in upward:
            copy.wait_recv()
        flux, tangent = edge(low[2], (low[0], low[1]), (press[0], step[0]))
        out_mr[0] = out_mr[0] - flux
        out_mp[0] = out_mp[0] - tangent

    @pl.when(me < peers - 1)
    def _():
        for copy in downward:
            copy.wait_recv()
        flux, tangent = edge(
            t_strike[nx - 1], (press[nx - 1], step[nx - 1]), (high[0], high[1])
        )
        out_mr[nx - 1] = out_mr[nx - 1] + flux
        out_mp[nx - 1] = out_mp[nx - 1] + tangent

    def take(off, carry):
        exchange(off, lax.rem(me + off, peers), lax.rem(me + peers - off, peers)).wait_recv()
        return carry

    lax.fori_loop(1, peers, take, 0, unroll=peers <= 16)

    got = recv[:, 0, :]
    got_fp, got_fd, got_tr, got_mp = (got[:, i * cap : (i + 1) * cap] for i in range(4))
    got_md = recv[:, 1, 0:cap]

    def link(trans, a, b):
        ea, eb = jnp.exp(COMPRESSIBILITY * a[0]), jnp.exp(COMPRESSIBILITY * b[0])
        return face(trans, a[0], b[0], a[1], b[1], ea, eb, ea * a[1], eb * b[1])

    m_flux, m_tangent = link(got_tr, (mp, md), (got_fp, got_fd))
    sums = scatter(pack(m_flux), pack(m_tangent), ones_of(m_row_masks), m_col_masks)
    out_mr[...] += unfold(sums[0])
    out_mp[...] += unfold(sums[1])
    f_flux, f_tangent = link(tr, (got_mp, got_md), (fp, fd))
    sums = scatter(pack(f_flux), pack(f_tangent), ones_of(f_row_masks), f_col_masks)
    out_fr[0] -= sums[0]
    out_fp[0] -= sums[1]

    def sent(off, carry):
        exchange(off, lax.rem(me + off, peers), me).wait_send()
        return carry

    lax.fori_loop(1, peers, sent, 0, unroll=peers <= 16)

    @pl.when(me < peers - 1)
    def _():
        for copy in upward:
            copy.wait_send()

    @pl.when(me > 0)
    def _():
        for copy in downward:
            copy.wait_send()


def per_device(peers, *args):
    nx, nz, ny = args[0].shape
    sems = lambda n: pltpu.SemaphoreType.DMA((n,))
    outs = [jax.ShapeDtypeStruct(args[i].shape, jnp.float32) for i in (0, 0, 7, 7)]
    spec = lambda space, n: [pl.BlockSpec(memory_space=space)] * n
    args = [pltpu.with_memory_space_constraint(x, pltpu.HBM) for x in args]
    results = pl.pallas_call(
        functools.partial(kernel, peers),
        out_shape=outs,
        in_specs=spec(pltpu.HBM, 17),
        out_specs=spec(pltpu.VMEM, 4),
        scratch_shapes=[pltpu.VMEM(x.shape, x.dtype) for x in args]
        + [
            pltpu.VMEM((peers, 2, LANES), jnp.float32),
            pltpu.VMEM((peers, 2, LANES), jnp.float32),
            pltpu.VMEM((3, nz, ny), jnp.float32),
            pltpu.VMEM((2, nz, ny), jnp.float32),
            sems(17),
            sems(peers),
            sems(peers),
            sems(5),
            sems(5),
        ],
        compiler_params=pltpu.CompilerParams(
            collective_id=0, has_side_effects=True, vmem_limit_bytes=32 * 1024 * 1024
        ),
    )(*args)
    return pl.pallas_call(
        store,
        out_shape=outs,
        in_specs=spec(pltpu.VMEM, 4),
        out_specs=spec(pltpu.HBM, 4),
        scratch_shapes=[sems(4)],
    )(*results)


def solution(mesh):
    three = P(("group", "strike"), None, None)
    two = P(("group", "strike"), None)
    return jax.shard_map(
        functools.partial(per_device, mesh.shape["strike"]),
        mesh=mesh,
        in_specs=(three,) * 13 + (two,) + (three,) * 3,
        out_specs=(three,) * 4,
        check_vma=False,
    )
```

```python
import functools

import jax
import jax.numpy as jnp
from jax import lax
from jax.experimental import pallas as pl
from jax.experimental.pallas import tpu as pltpu
from jax.sharding import PartitionSpec as P

COMPRESSIBILITY = 0.5
LANES = 128
MESH = pl.DeviceIdType.MESH


def face(trans, pa, pb, da, db, ea, eb, ga, gb):
    drop = pa - pb
    total = 0.5 * trans * (ea + eb)
    flux = total * drop
    tangent = (0.25 * trans) * (ga + gb) * drop + total * (da - db)
    return flux, tangent


def shift_faces(resid, linear, trans, p, d, e, g, axis):
    size = p.shape[axis]
    here = lax.broadcasted_iota(jnp.int32, p.shape, axis)
    trans = jnp.where(here < size - 1, trans, 0.0)
    up = lambda x: pltpu.roll(x, size - 1, axis)
    down = lambda x: pltpu.roll(x, 1, axis)
    flux, tangent = face(trans, p, up(p), d, up(d), e, up(e), g, up(g))
    return resid + flux - down(flux), linear + tangent - down(tangent)


def split(x, terms):
    out = []
    for _ in range(terms):
        head = x.astype(jnp.bfloat16)
        out.append(head)
        x = x - head.astype(jnp.float32)
    return out


def pack(x):
    fold = LANES // x.shape[1]
    n = x.shape[0] // fold
    return jnp.concatenate([x[b * n : (b + 1) * n] for b in range(fold)], axis=1)


def unpack(x, width):
    fold = LANES // width
    return jnp.concatenate([x[:, b * width : (b + 1) * width] for b in range(fold)], axis=0)


def wide(rows, ref_rows):
    iota = lax.broadcasted_iota(jnp.int32, (ref_rows, LANES), 0)
    return [iota == rows[a : a + 1, :] for a in range(rows.shape[0])]


def ones_of(masks):
    return jnp.concatenate(
        [jnp.where(m, 1.0, 0.0).astype(jnp.bfloat16) for m in masks], axis=1
    )


def gather(first, second, row_masks, col_ones):
    size = first.shape[0]
    lhs = jnp.concatenate(
        [jnp.concatenate(split(x, 3), axis=1) for x in (first, second)], axis=0
    )
    rhs = jnp.concatenate([col_ones] * 3, axis=0)
    found = jnp.dot(lhs, rhs, preferred_element_type=jnp.float32)
    out = []
    for q in range(2):
        rows = []
        for a, mask in enumerate(row_masks):
            block = found[q * size : (q + 1) * size, a * LANES : (a + 1) * LANES]
            rows.append(jnp.sum(jnp.where(mask, block, 0.0), axis=0, keepdims=True))
        out.append(jnp.concatenate(rows, axis=0))
    return out


def scatter(first, second, row_ones, col_masks):
    def weights(part):
        stacked = []
        for rows in part:
            stacked.append(
                jnp.concatenate(
                    [
                        jnp.where(mask, rows[a : a + 1, :].astype(jnp.float32), 0.0).astype(
                            jnp.bfloat16
                        )
                        for a, mask in enumerate(col_masks)
                    ],
                    axis=1,
                )
            )
        return jnp.concatenate(stacked, axis=1)

    rhs = jnp.concatenate([weights(split(first, 2)), weights(split(second, 2))], axis=0)
    lhs = jnp.concatenate([row_ones] * 2, axis=1)
    sums = lax.dot_general(
        lhs, rhs, (((1,), (1,)), ((), ())), preferred_element_type=jnp.float32
    )
    return sums[:, :LANES], sums[:, LANES:]


def store(*refs):
    n = (len(refs) - 1) // 2
    copies = [
        pltpu.make_async_copy(refs[i], refs[n + i], refs[-1].at[i]) for i in range(n)
    ]
    for copy in copies:
        copy.start()
    for copy in copies:
        copy.wait()


def kernel(peers, *refs):
    ins, outs, scratch = refs[:17], refs[17:21], refs[21:]
    bufs = scratch[:17]
    m_ones, f_ones, send, recv, low, high, load_sem, send_sem, recv_sem, halo_send, halo_recv = scratch[17:]
    me = lax.axis_index("strike")
    load = [
        pltpu.make_async_copy(ins[i], bufs[i], load_sem.at[i]) for i in range(17)
    ]
    order = (16, 15, 0, 1, 7, 8, 13, 14, 2, 3, 4, 5, 6, 9, 10, 11, 12)
    for i in order[:8]:
        load[i].start()

    barrier = pltpu.get_barrier_semaphore()

    def greet(off, carry):
        pl.semaphore_signal(
            barrier, 1, device_id={"strike": lax.rem(me + off, peers)}, device_id_type=MESH
        )
        return carry

    lax.fori_loop(1, peers, greet, 0, unroll=peers <= 16)
    for i in order[8:]:
        load[i].start()

    (press, step, pore, old, t_strike, t_layer, t_dip) = bufs[:7]
    (f_press, f_step, f_volume, f_old, f_along, f_across) = bufs[7:13]
    count, c_trans, f_index, m_index = bufs[13:]
    nx, nz, ny = press.shape
    side = f_press.shape[1]
    rows_m = nx * nz
    cols = ny // LANES
    cap = c_trans.shape[2]

    def fold(x):
        flat = x.reshape(rows_m, ny)
        return jnp.concatenate(
            [flat[:, j * LANES : (j + 1) * LANES] for j in range(cols)], axis=0
        )

    def unfold(x):
        flat = jnp.concatenate(
            [x[j * rows_m : (j + 1) * rows_m] for j in range(cols)], axis=1
        )
        return flat.reshape(nx, nz, ny)

    for i in (16, 0, 1):
        load[i].wait()
    cell = pack(m_index[0])
    along = cell & (ny - 1)
    m_row = (along >> 7) * rows_m + (cell >> (ny.bit_length() - 1))
    m_col = along & (LANES - 1)
    m_row_masks = wide(m_row, rows_m * cols)
    m_col_masks = wide(m_col, LANES)
    mp, md = gather(fold(press[...]), fold(step[...]), m_row_masks, ones_of(m_col_masks))
    mp, md = unpack(mp, cap), unpack(md, cap)

    for i in (15, 7, 8):
        load[i].wait()
    cell = pack(f_index[0])
    f_row = cell >> 7
    f_col = cell & (LANES - 1)
    f_row_masks = wide(f_row, side)
    f_col_masks = wide(f_col, LANES)
    fp, fd = gather(f_press[0], f_step[0], f_row_masks, ones_of(f_col_masks))
    fp, fd = unpack(fp, cap), unpack(fd, cap)

    for i in (13, 14):
        load[i].wait()
    diagonal = lax.broadcasted_iota(jnp.int32, (peers, peers), 0) == lax.broadcasted_iota(
        jnp.int32, (peers, peers), 1
    )
    limit = jnp.sum(
        jnp.where(diagonal, count[...].astype(jnp.float32), 0.0), axis=1, keepdims=True
    )
    slot = lax.broadcasted_iota(jnp.int32, (peers, cap), 1).astype(jnp.float32)
    tr = jnp.where(slot < limit, c_trans[0], 0.0)

    first = jnp.concatenate([fp, fd, tr, mp], axis=1)
    send[:, 0, :] = first
    send[:, 1, :] = jnp.concatenate([md, jnp.zeros((peers, LANES - cap), jnp.float32)], axis=1)

    pl.semaphore_wait(barrier, peers - 1)

    def exchange(off, to, slot_there):
        return pltpu.make_async_remote_copy(
            src_ref=send.at[to],
            dst_ref=recv.at[slot_there],
            send_sem=send_sem.at[off],
            recv_sem=recv_sem.at[off],
            device_id={"strike": to},
            device_id_type=MESH,
        )

    def push(off, carry):
        exchange(off, lax.rem(me + off, peers), me).start()
        return carry

    lax.fori_loop(1, peers, push, 0, unroll=peers <= 16)

    following = lax.rem(me + 1, peers)
    previous = lax.rem(me + peers - 1, peers)

    load[4].wait()
    upward = [
        pltpu.make_async_remote_copy(
            src_ref=x.at[nx - 1],
            dst_ref=low.at[i],
            send_sem=halo_send.at[i],
            recv_sem=halo_recv.at[i],
            device_id={"strike": following},
            device_id_type=MESH,
        )
        for i, x in enumerate((press, step, t_strike))
    ]
    downward = [
        pltpu.make_async_remote_copy(
            src_ref=x.at[0],
            dst_ref=high.at[i],
            send_sem=halo_send.at[3 + i],
            recv_sem=halo_recv.at[3 + i],
            device_id={"strike": previous},
            device_id_type=MESH,
        )
        for i, x in enumerate((press, step))
    ]

    @pl.when(me < peers - 1)
    def _():
        for copy in upward:
            copy.start()

    @pl.when(me > 0)
    def _():
        for copy in downward:
            copy.start()

    recv[me] = send[me]

    for i in (2, 3, 5, 6, 9, 10, 11, 12):
        load[i].wait()

    out_mr, out_mp, out_fr, out_fp = outs
    m_ones[...] = ones_of(m_row_masks)
    f_ones[...] = ones_of(f_row_masks)

    p, d = press[...], step[...]
    e = jnp.exp(COMPRESSIBILITY * p)
    g = e * d
    resid = pore[...] * e - old[...]
    linear = pore[...] * COMPRESSIBILITY * g
    for axis, trans in ((1, t_layer), (2, t_dip)):
        resid, linear = shift_faces(resid, linear, trans[...], p, d, e, g, axis)
    planes_r = [resid[i] for i in range(nx)]
    planes_l = [linear[i] for i in range(nx)]
    for i in range(nx - 1):
        flux, tangent = face(
            t_strike[i], p[i], p[i + 1], d[i], d[i + 1], e[i], e[i + 1], g[i], g[i + 1]
        )
        planes_r[i] = planes_r[i] + flux
        planes_l[i] = planes_l[i] + tangent
        planes_r[i + 1] = planes_r[i + 1] - flux
        planes_l[i + 1] = planes_l[i + 1] - tangent
    for i in range(nx):
        out_mr[i] = planes_r[i]
        out_mp[i] = planes_l[i]

    q, w = f_press[0], f_step[0]
    h = jnp.exp(COMPRESSIBILITY * q)
    k = h * w
    f_resid = f_volume[0] * h - f_old[0]
    f_linear = f_volume[0] * COMPRESSIBILITY * k
    for axis, trans in ((0, f_along), (1, f_across)):
        f_resid, f_linear = shift_faces(f_resid, f_linear, trans[0], q, w, h, k, axis)
    out_fr[0] = f_resid
    out_fp[0] = f_linear

    def edge(trans, a, b):
        return face(
            trans,
            a[0],
            b[0],
            a[1],
            b[1],
            jnp.exp(COMPRESSIBILITY * a[0]),
            jnp.exp(COMPRESSIBILITY * b[0]),
            jnp.exp(COMPRESSIBILITY * a[0]) * a[1],
            jnp.exp(COMPRESSIBILITY * b[0]) * b[1],
        )

    @pl.when(me > 0)
    def _():
        for copy in upward:
            copy.wait_recv()
        flux, tangent = edge(low[2], (low[0], low[1]), (press[0], step[0]))
        out_mr[0] = out_mr[0] - flux
        out_mp[0] = out_mp[0] - tangent

    @pl.when(me < peers - 1)
    def _():
        for copy in downward:
            copy.wait_recv()
        flux, tangent = edge(
            t_strike[nx - 1], (press[nx - 1], step[nx - 1]), (high[0], high[1])
        )
        out_mr[nx - 1] = out_mr[nx - 1] + flux
        out_mp[nx - 1] = out_mp[nx - 1] + tangent

    def take(off, carry):
        exchange(off, lax.rem(me + off, peers), lax.rem(me + peers - off, peers)).wait_recv()
        return carry

    lax.fori_loop(1, peers, take, 0, unroll=peers <= 16)

    got = recv[:, 0, :]
    got_fp, got_fd, got_tr, got_mp = (got[:, i * cap : (i + 1) * cap] for i in range(4))
    got_md = recv[:, 1, 0:cap]

    def link(trans, a, b):
        ea, eb = jnp.exp(COMPRESSIBILITY * a[0]), jnp.exp(COMPRESSIBILITY * b[0])
        return face(trans, a[0], b[0], a[1], b[1], ea, eb, ea * a[1], eb * b[1])

    m_flux, m_tangent = link(got_tr, (mp, md), (got_fp, got_fd))
    sums = scatter(pack(m_flux), pack(m_tangent), m_ones[...], m_col_masks)
    out_mr[...] += unfold(sums[0])
    out_mp[...] += unfold(sums[1])
    f_flux, f_tangent = link(tr, (got_mp, got_md), (fp, fd))
    sums = scatter(pack(f_flux), pack(f_tangent), f_ones[...], f_col_masks)
    out_fr[0] -= sums[0]
    out_fp[0] -= sums[1]

    def sent(off, carry):
        exchange(off, lax.rem(me + off, peers), me).wait_send()
        return carry

    lax.fori_loop(1, peers, sent, 0, unroll=peers <= 16)

    @pl.when(me < peers - 1)
    def _():
        for copy in upward:
            copy.wait_send()

    @pl.when(me > 0)
    def _():
        for copy in downward:
            copy.wait_send()


def per_device(peers, *args):
    nx, nz, ny = args[0].shape
    slots = peers * args[14].shape[2]
    sems = lambda n: pltpu.SemaphoreType.DMA((n,))
    outs = [jax.ShapeDtypeStruct(args[i].shape, jnp.float32) for i in (0, 0, 7, 7)]
    spec = lambda space, n: [pl.BlockSpec(memory_space=space)] * n
    args = [pltpu.with_memory_space_constraint(x, pltpu.HBM) for x in args]
    results = pl.pallas_call(
        functools.partial(kernel, peers),
        out_shape=outs,
        in_specs=spec(pltpu.HBM, 17),
        out_specs=spec(pltpu.VMEM, 4),
        scratch_shapes=[pltpu.VMEM(x.shape, x.dtype) for x in args]
        + [
            pltpu.VMEM((nx * nz * ny // LANES, slots), jnp.bfloat16),
            pltpu.VMEM((args[7].shape[1], slots), jnp.bfloat16),
            pltpu.VMEM((peers, 2, LANES), jnp.float32),
            pltpu.VMEM((peers, 2, LANES), jnp.float32),
            pltpu.VMEM((3, nz, ny), jnp.float32),
            pltpu.VMEM((2, nz, ny), jnp.float32),
            sems(17),
            sems(peers),
            sems(peers),
            sems(5),
            sems(5),
        ],
        compiler_params=pltpu.CompilerParams(
            collective_id=0, has_side_effects=True, vmem_limit_bytes=32 * 1024 * 1024
        ),
    )(*args)
    return pl.pallas_call(
        store,
        out_shape=outs,
        in_specs=spec(pltpu.VMEM, 4),
        out_specs=spec(pltpu.HBM, 4),
        scratch_shapes=[sems(4)],
        compiler_params=pltpu.CompilerParams(vmem_limit_bytes=4 * 1024 * 1024),
    )(*results)


def solution(mesh):
    three = P(("group", "strike"), None, None)
    two = P(("group", "strike"), None)
    return jax.shard_map(
        functools.partial(per_device, mesh.shape["strike"]),
        mesh=mesh,
        in_specs=(three,) * 13 + (two,) + (three,) * 3,
        out_specs=(three,) * 4,
        check_vma=False,
    )
```

```python
import functools

import jax
import jax.numpy as jnp
from jax import lax
from jax.experimental import pallas as pl
from jax.experimental.pallas import tpu as pltpu
from jax.sharding import PartitionSpec as P

COMPRESSIBILITY = 0.5
LANES = 128
MESH = pl.DeviceIdType.MESH


def face(trans, pa, pb, da, db, ea, eb, ga, gb):
    drop = pa - pb
    total = 0.5 * trans * (ea + eb)
    flux = total * drop
    tangent = (0.25 * trans) * (ga + gb) * drop + total * (da - db)
    return flux, tangent


def shift_faces(resid, linear, trans, p, d, e, g, axis):
    size = p.shape[axis]
    here = lax.broadcasted_iota(jnp.int32, p.shape, axis)
    trans = jnp.where(here < size - 1, trans, 0.0)
    up = lambda x: pltpu.roll(x, size - 1, axis)
    down = lambda x: pltpu.roll(x, 1, axis)
    flux, tangent = face(trans, p, up(p), d, up(d), e, up(e), g, up(g))
    return resid + flux - down(flux), linear + tangent - down(tangent)


def split(x, terms):
    out = []
    for _ in range(terms):
        head = x.astype(jnp.bfloat16)
        out.append(head)
        x = x - head.astype(jnp.float32)
    return out


def pack(x):
    fold = LANES // x.shape[1]
    n = x.shape[0] // fold
    return jnp.concatenate([x[b * n : (b + 1) * n] for b in range(fold)], axis=1)


def unpack(x, width):
    fold = LANES // width
    return jnp.concatenate([x[:, b * width : (b + 1) * width] for b in range(fold)], axis=0)


def wide(rows, ref_rows):
    iota = lax.broadcasted_iota(jnp.int32, (ref_rows, LANES), 0)
    return [iota == rows[a : a + 1, :] for a in range(rows.shape[0])]


def ones_of(masks):
    return jnp.concatenate(
        [jnp.where(m, 1.0, 0.0).astype(jnp.bfloat16) for m in masks], axis=1
    )


def gather(first, second, row_masks, col_ones):
    size = first.shape[0]
    lhs = jnp.concatenate(
        [jnp.concatenate(split(x, 2), axis=1) for x in (first, second)], axis=0
    )
    rhs = jnp.concatenate([col_ones] * 2, axis=0)
    found = jnp.dot(lhs, rhs, preferred_element_type=jnp.float32)
    out = []
    for q in range(2):
        rows = []
        for a, mask in enumerate(row_masks):
            block = found[q * size : (q + 1) * size, a * LANES : (a + 1) * LANES]
            rows.append(jnp.sum(jnp.where(mask, block, 0.0), axis=0, keepdims=True))
        out.append(jnp.concatenate(rows, axis=0))
    return out


def scatter(first, second, row_ones, col_masks):
    def weights(part):
        stacked = []
        for rows in part:
            stacked.append(
                jnp.concatenate(
                    [
                        jnp.where(mask, rows[a : a + 1, :].astype(jnp.float32), 0.0).astype(
                            jnp.bfloat16
                        )
                        for a, mask in enumerate(col_masks)
                    ],
                    axis=1,
                )
            )
        return jnp.concatenate(stacked, axis=1)

    rhs = jnp.concatenate([weights(split(first, 2)), weights(split(second, 2))], axis=0)
    lhs = jnp.concatenate([row_ones] * 2, axis=1)
    sums = lax.dot_general(
        lhs, rhs, (((1,), (1,)), ((), ())), preferred_element_type=jnp.float32
    )
    return sums[:, :LANES], sums[:, LANES:]


def store(*refs):
    n = (len(refs) - 1) // 2
    copies = [
        pltpu.make_async_copy(refs[i], refs[n + i], refs[-1].at[i]) for i in range(n)
    ]
    for copy in copies:
        copy.start()
    for copy in copies:
        copy.wait()


def kernel(peers, *refs):
    ins, outs, scratch = refs[:17], refs[17:21], refs[21:]
    bufs = scratch[:17]
    m_ones, f_ones, send, recv, low, high, load_sem, send_sem, recv_sem, halo_send, halo_recv = scratch[17:]
    me = lax.axis_index("strike")

    def wrap(x):
        return jnp.where(x >= peers, x - peers, x)

    load = [
        pltpu.make_async_copy(ins[i], bufs[i], load_sem.at[i]) for i in range(17)
    ]
    order = (16, 15, 0, 1, 7, 8, 13, 14, 2, 3, 4, 5, 6, 9, 10, 11, 12)
    for i in order[:8]:
        load[i].start()

    barrier = pltpu.get_barrier_semaphore()

    def greet(off, carry):
        pl.semaphore_signal(
            barrier, 1, device_id={"strike": wrap(me + off)}, device_id_type=MESH
        )
        return carry

    lax.fori_loop(1, peers, greet, 0, unroll=peers <= 16)
    (press, step, pore, old, t_strike, t_layer, t_dip) = bufs[:7]
    (f_press, f_step, f_volume, f_old, f_along, f_across) = bufs[7:13]
    count, c_trans, f_index, m_index = bufs[13:]
    nx, nz, ny = press.shape
    side = f_press.shape[1]
    rows_m = nx * nz
    cols = ny // LANES
    cap = c_trans.shape[2]

    def fold(x):
        flat = x.reshape(rows_m, ny)
        return jnp.concatenate(
            [flat[:, j * LANES : (j + 1) * LANES] for j in range(cols)], axis=0
        )

    def unfold(x):
        flat = jnp.concatenate(
            [x[j * rows_m : (j + 1) * rows_m] for j in range(cols)], axis=1
        )
        return flat.reshape(nx, nz, ny)

    for i in order[:8]:
        load[i].wait()
    cell = pack(m_index[0])
    along = cell & (ny - 1)
    m_row = (along >> 7) * rows_m + (cell >> (ny.bit_length() - 1))
    m_col = along & (LANES - 1)
    m_row_masks = wide(m_row, rows_m * cols)
    m_col_masks = wide(m_col, LANES)
    mp, md = gather(fold(press[...]), fold(step[...]), m_row_masks, ones_of(m_col_masks))
    mp, md = unpack(mp, cap), unpack(md, cap)

    cell = pack(f_index[0])
    f_row = cell >> 7
    f_col = cell & (LANES - 1)
    f_row_masks = wide(f_row, side)
    f_col_masks = wide(f_col, LANES)
    fp, fd = gather(f_press[0], f_step[0], f_row_masks, ones_of(f_col_masks))
    fp, fd = unpack(fp, cap), unpack(fd, cap)

    diagonal = lax.broadcasted_iota(jnp.int32, (peers, peers), 0) == lax.broadcasted_iota(
        jnp.int32, (peers, peers), 1
    )
    limit = jnp.sum(
        jnp.where(diagonal, count[...].astype(jnp.float32), 0.0), axis=1, keepdims=True
    )
    slot = lax.broadcasted_iota(jnp.int32, (peers, cap), 1).astype(jnp.float32)
    tr = jnp.where(slot < limit, c_trans[0], 0.0)

    first = jnp.concatenate([fp, fd, tr, mp], axis=1)
    send[:, 0, :] = first
    send[:, 1, :] = jnp.concatenate([md, jnp.zeros((peers, LANES - cap), jnp.float32)], axis=1)

    pl.semaphore_wait(barrier, peers - 1)

    def exchange(off, to, slot_there):
        return pltpu.make_async_remote_copy(
            src_ref=send.at[to],
            dst_ref=recv.at[slot_there],
            send_sem=send_sem.at[0],
            recv_sem=recv_sem.at[0],
            device_id={"strike": to},
            device_id_type=MESH,
        )

    def push(off, carry):
        exchange(off, wrap(me + off), me).start()
        return carry

    lax.fori_loop(1, peers, push, 0, unroll=peers <= 16)

    for i in order[8:]:
        load[i].start()

    following = wrap(me + 1)
    previous = wrap(me + peers - 1)

    load[4].wait()
    upward = [
        pltpu.make_async_remote_copy(
            src_ref=x.at[nx - 1],
            dst_ref=low.at[i],
            send_sem=halo_send.at[i],
            recv_sem=halo_recv.at[i],
            device_id={"strike": following},
            device_id_type=MESH,
        )
        for i, x in enumerate((press, step, t_strike))
    ]
    downward = [
        pltpu.make_async_remote_copy(
            src_ref=x.at[0],
            dst_ref=high.at[i],
            send_sem=halo_send.at[3 + i],
            recv_sem=halo_recv.at[3 + i],
            device_id={"strike": previous},
            device_id_type=MESH,
        )
        for i, x in enumerate((press, step))
    ]

    @pl.when(me < peers - 1)
    def _():
        for copy in upward:
            copy.start()

    @pl.when(me > 0)
    def _():
        for copy in downward:
            copy.start()

    everything = pltpu.make_async_remote_copy(
        src_ref=send.at[pl.ds(0, peers - 1)],
        dst_ref=recv.at[pl.ds(0, peers - 1)],
        send_sem=send_sem.at[0],
        recv_sem=recv_sem.at[0],
        device_id={"strike": following},
        device_id_type=MESH,
    )
    recv[me] = send[me]

    for i in (2, 3, 5, 6, 9, 10, 11, 12):
        load[i].wait()

    out_mr, out_mp, out_fr, out_fp = outs
    m_ones[...] = ones_of(m_row_masks)
    f_ones[...] = ones_of(f_row_masks)

    p, d = press[...], step[...]
    e = jnp.exp(COMPRESSIBILITY * p)
    g = e * d
    resid = pore[...] * e - old[...]
    linear = pore[...] * COMPRESSIBILITY * g
    for axis, trans in ((1, t_layer), (2, t_dip)):
        resid, linear = shift_faces(resid, linear, trans[...], p, d, e, g, axis)
    planes_r = [resid[i] for i in range(nx)]
    planes_l = [linear[i] for i in range(nx)]
    for i in range(nx - 1):
        flux, tangent = face(
            t_strike[i], p[i], p[i + 1], d[i], d[i + 1], e[i], e[i + 1], g[i], g[i + 1]
        )
        planes_r[i] = planes_r[i] + flux
        planes_l[i] = planes_l[i] + tangent
        planes_r[i + 1] = planes_r[i + 1] - flux
        planes_l[i + 1] = planes_l[i + 1] - tangent
    for i in range(nx):
        out_mr[i] = planes_r[i]
        out_mp[i] = planes_l[i]

    q, w = f_press[0], f_step[0]
    h = jnp.exp(COMPRESSIBILITY * q)
    k = h * w
    f_resid = f_volume[0] * h - f_old[0]
    f_linear = f_volume[0] * COMPRESSIBILITY * k
    for axis, trans in ((0, f_along), (1, f_across)):
        f_resid, f_linear = shift_faces(f_resid, f_linear, trans[0], q, w, h, k, axis)
    out_fr[0] = f_resid
    out_fp[0] = f_linear

    def edge(trans, a, b):
        return face(
            trans,
            a[0],
            b[0],
            a[1],
            b[1],
            jnp.exp(COMPRESSIBILITY * a[0]),
            jnp.exp(COMPRESSIBILITY * b[0]),
            jnp.exp(COMPRESSIBILITY * a[0]) * a[1],
            jnp.exp(COMPRESSIBILITY * b[0]) * b[1],
        )

    @pl.when(me > 0)
    def _():
        for copy in upward:
            copy.wait_recv()
        flux, tangent = edge(low[2], (low[0], low[1]), (press[0], step[0]))
        out_mr[0] = out_mr[0] - flux
        out_mp[0] = out_mp[0] - tangent

    @pl.when(me < peers - 1)
    def _():
        for copy in downward:
            copy.wait_recv()
        flux, tangent = edge(
            t_strike[nx - 1], (press[nx - 1], step[nx - 1]), (high[0], high[1])
        )
        out_mr[nx - 1] = out_mr[nx - 1] + flux
        out_mp[nx - 1] = out_mp[nx - 1] + tangent

    everything.wait_recv()

    got = recv[:, 0, :]
    got_fp, got_fd, got_tr, got_mp = (got[:, i * cap : (i + 1) * cap] for i in range(4))
    got_md = recv[:, 1, 0:cap]

    def link(trans, a, b):
        ea, eb = jnp.exp(COMPRESSIBILITY * a[0]), jnp.exp(COMPRESSIBILITY * b[0])
        return face(trans, a[0], b[0], a[1], b[1], ea, eb, ea * a[1], eb * b[1])

    m_flux, m_tangent = link(got_tr, (mp, md), (got_fp, got_fd))
    sums = scatter(pack(m_flux), pack(m_tangent), m_ones[...], m_col_masks)
    out_mr[...] += unfold(sums[0])
    out_mp[...] += unfold(sums[1])
    f_flux, f_tangent = link(tr, (got_mp, got_md), (fp, fd))
    sums = scatter(pack(f_flux), pack(f_tangent), f_ones[...], f_col_masks)
    out_fr[0] -= sums[0]
    out_fp[0] -= sums[1]

    everything.wait_send()

    @pl.when(me < peers - 1)
    def _():
        for copy in upward:
            copy.wait_send()

    @pl.when(me > 0)
    def _():
        for copy in downward:
            copy.wait_send()


def per_device(peers, *args):
    nx, nz, ny = args[0].shape
    slots = peers * args[14].shape[2]
    sems = lambda n: pltpu.SemaphoreType.DMA((n,))
    outs = [jax.ShapeDtypeStruct(args[i].shape, jnp.float32) for i in (0, 0, 7, 7)]
    spec = lambda space, n: [pl.BlockSpec(memory_space=space)] * n
    args = [pltpu.with_memory_space_constraint(x, pltpu.HBM) for x in args]
    results = pl.pallas_call(
        functools.partial(kernel, peers),
        out_shape=outs,
        in_specs=spec(pltpu.HBM, 17),
        out_specs=spec(pltpu.VMEM, 4),
        scratch_shapes=[pltpu.VMEM(x.shape, x.dtype) for x in args]
        + [
            pltpu.VMEM((nx * nz * ny // LANES, slots), jnp.bfloat16),
            pltpu.VMEM((args[7].shape[1], slots), jnp.bfloat16),
            pltpu.VMEM((peers, 2, LANES), jnp.float32),
            pltpu.VMEM((peers, 2, LANES), jnp.float32),
            pltpu.VMEM((3, nz, ny), jnp.float32),
            pltpu.VMEM((2, nz, ny), jnp.float32),
            sems(17),
            sems(1),
            sems(1),
            sems(5),
            sems(5),
        ],
        compiler_params=pltpu.CompilerParams(
            collective_id=0, has_side_effects=True, vmem_limit_bytes=32 * 1024 * 1024
        ),
    )(*args)
    return pl.pallas_call(
        store,
        out_shape=outs,
        in_specs=spec(pltpu.VMEM, 4),
        out_specs=spec(pltpu.HBM, 4),
        scratch_shapes=[sems(4)],
        compiler_params=pltpu.CompilerParams(vmem_limit_bytes=4 * 1024 * 1024),
    )(*results)


def solution(mesh):
    three = P(("group", "strike"), None, None)
    two = P(("group", "strike"), None)
    return jax.shard_map(
        functools.partial(per_device, mesh.shape["strike"]),
        mesh=mesh,
        in_specs=(three,) * 13 + (two,) + (three,) * 3,
        out_specs=(three,) * 4,
        check_vma=False,
    )
```
